512 devices in a mesh: blk: 32 (over z_lo, y, core), head: 16 (over z_hi, x).
Axes of the slice: x: 4, y: 4, z: 16 (z_hi: 4, z_lo: 4; z = z_hi * 4 + z_lo), core: 2. Of those that a mesh axis runs over, the one named last changes fastest.
Arguments:
- queries: bfloat16 [65536, 2048], P(('blk', 'head')), may hold values from -300 to 300
- keys: bfloat16 [65536, 1024], P(('blk', 'head')), may hold values from -6 to 6
- values: bfloat16 [65536, 1024], P(('blk', 'head')), may hold values from -6 to 6
Outputs:
- context: bfloat16 [65536, 2048], P(('blk', 'head'))
The draws below stay inside these ranges and needn't reach their ends.
All inputs are finite; a program needn't handle non-finite values.
Results may differ from the reference program's by a relative error of at most 0.0095.
Values may be sent and summed in bfloat16 or wider, within the bound.
No kernel may reach another device: no remote copies, remote signals or barrier semaphores. Data moves between devices by JAX's collectives and lax.ppermute only.
A program may use at most 64 MiB of HBM per device.

```python
import jax
import jax.numpy as jnp
from jax import lax

QH = 16
KVH = 8
HD = 128
BLOCK = 2048
TOKENS = 65536


def shared_keys(key):
    base = jax.random.fold_in(key, 11)
    normal_part = jnp.clip(jax.random.normal(base, (TOKENS, KVH * HD), jnp.float32), -6.0, 6.0)
    return normal_part


def draw_keys(key, part):
    result = shared_keys(key)
    return result.astype(jnp.bfloat16)


def draw_queries(key, part):
    own_key = jax.random.fold_in(key, 12)
    normal_part = jnp.clip(jax.random.normal(own_key, (TOKENS, QH * HD), jnp.float32), -6.0, 6.0)
    result = normal_part
    return result.astype(jnp.bfloat16)


def steps_of(stream_key, dims, shards, low, largest):
    loudness, own = 1.0, jax.random.fold_in(stream_key, 6)
    for dim, shards_of in shards:
        heights = jnp.exp(jax.random.uniform(jax.random.fold_in(own, dim), (shards_of,), jnp.float32, low / len(shards), largest / len(shards)))
        loudness = loudness * jnp.repeat(heights, dims[dim] // shards_of).reshape([-1 if axis == dim else 1 for axis in range(len(dims))])
    return loudness


def scatter_about(key, dims, spread, reach, pieces=(), held_as=jnp.bfloat16):
    values = spread * jax.random.normal(key, dims, jnp.float32)
    if pieces:
        values = values * steps_of(key, dims, pieces, -0.22, 0.18)
    return jnp.clip(values, -reach, reach).astype(held_as)


def setup_inputs(seed: int = 0) -> dict:
    arg_keys = jax.random.split(jax.random.key(seed), 4)
    return {
        "queries": draw_queries(jax.random.fold_in(arg_keys[3], 71), 0),
        "keys": draw_keys(jax.random.fold_in(arg_keys[3], 71), 0),
        "values": scatter_about(arg_keys[2], (TOKENS, KVH * HD), 1.0, 6.0, ((0, 512),)),
    }


def reference(queries, keys, values):
    blocks = TOKENS // BLOCK
    group = QH // KVH
    q_all = queries.reshape(blocks, BLOCK, KVH, group, HD)
    k_all = keys.reshape(blocks, BLOCK, KVH, HD)
    v_all = values.reshape(blocks, BLOCK, KVH, HD)
    causal = jnp.tril(jnp.ones((BLOCK, BLOCK), dtype=bool))

    def one_block(index):
        q_here = q_all[index]
        k_here = jnp.concatenate([k_all[0], k_all[index]], 0)
        v_here = jnp.concatenate([v_all[0], v_all[index]], 0)
        allowed = jnp.concatenate([jnp.broadcast_to(index > 0, (BLOCK, BLOCK)), causal], 1)

        def one_head(head):
            q_head = q_here[:, head].astype(jnp.float32)
            k_head = k_here[:, head].astype(jnp.float32)
            v_head = v_here[:, head].astype(jnp.float32)
            scores = jnp.einsum("qgd,sd->gqs", q_head, k_head) * (HD ** -0.5)
            scores = jnp.where(allowed, scores, jnp.float32(-1.0e30))
            peak = jnp.max(scores, axis=-1, keepdims=True)
            expo = jnp.exp(scores - peak)
            total = jnp.sum(expo, axis=-1)
            weights = expo.astype(jnp.bfloat16).astype(jnp.float32)
            mixed = jnp.einsum("gqs,sd->gqd", weights, v_head) / total[..., None]
            return mixed.astype(jnp.bfloat16)

        heads = lax.map(one_head, jnp.arange(KVH))
        return heads.transpose(2, 0, 1, 3).reshape(BLOCK, QH * HD)

    return lax.map(one_block, jnp.arange(blocks)).reshape(TOKENS, QH * HD)
```

```python
import functools

import jax
import jax.numpy as jnp
from jax import lax
from jax.experimental import pallas as pl
from jax.experimental.pallas import tpu as pltpu
from jax.sharding import PartitionSpec as P

HD = 128
BF = jnp.bfloat16
F32 = jnp.float32
masked_value = -1e30
exp2_scale = 0.08838834764831845 * 1.4426950408889634

ZL, YY, CC, ZH, XX = 4, 4, 2, 4, 4


def device_index(zl, y, c, zh, x):
    return ((zl * YY + y) * CC + c) * (ZH * XX) + zh * XX + x


def pairs(move):
    found = []
    for zl in range(ZL):
        for y in range(YY):
            for c in range(CC):
                for zh in range(ZH):
                    for x in range(XX):
                        to = move(zl, y, c, zh, x)
                        if to is not None:
                            found.append((device_index(zl, y, c, zh, x), device_index(*to)))
    return found


def send(block, move):
    return lax.ppermute(block, ("blk", "head"), pairs(move))


def absorb_tile(q, k, v, state, keep=None):
    peak, total, summed = state
    scores = lax.dot_general(k, q, (((1,), (1,)), ((), ())), preferred_element_type=F32)
    if keep is not None:
        scores = jnp.where(keep, scores, masked_value)
    new_peak = jnp.maximum(peak, jnp.max(scores, axis=0, keepdims=True))
    expo = jnp.exp2((scores - new_peak) * exp2_scale)
    rescale = jnp.exp2((peak - new_peak) * exp2_scale)
    total = total * rescale + jnp.sum(expo, axis=0, keepdims=True)
    summed = summed * rescale + lax.dot_general(
        v, expo.astype(BF), (((0,), (0,)), ((), ())), preferred_element_type=F32
    )
    return new_peak, total, summed


def absorb_pair(refs, q_ref, k, v, keep=None, start=None):
    for g in range(2):
        q = q_ref[:, g * HD : (g + 1) * HD]
        state = start or tuple(ref[g] for ref in refs)
        for ref, part in zip(refs, absorb_tile(q, k, v, state, keep)):
            ref[g] = part


def own_kernel(where_ref, q_ref, ok, ov, *outs):
    refs, where_out = outs[:3], outs[3]
    x = where_ref[0]
    for n in range(3):
        where_out[n] = where_ref[n]
    rows = q_ref.shape[0]

    def place(r):
        return jnp.bitwise_and(x + XX - r // 128, XX - 1) * 128 + r % 128

    key_at = place(lax.broadcasted_iota(jnp.int32, (rows, rows), 0))
    query_at = place(lax.broadcasted_iota(jnp.int32, (rows, rows), 1))
    start = (
        jnp.full((1, rows), masked_value, F32),
        jnp.zeros((1, rows), F32),
        jnp.zeros((HD, rows), F32),
    )
    absorb_pair(refs, q_ref, ok[...], ov[...], key_at <= query_at, start)


def middle_kernel(where_ref, q_ref, p_ref, t_ref, s_ref, ak, av, bk, bv, nk, nv, *refs):
    zh, blk = where_ref[1], where_ref[2]
    for ref, before in zip(refs, (p_ref, t_ref, s_ref)):
        ref[...] = before[...]

    @pl.when(blk > 0)
    def _():
        tile = 512

        def step(t, _):
            at = pl.ds(pl.multiple_of(t * tile, tile), tile)
            absorb_pair(refs, q_ref, nk[at, :], nv[at, :])
            return 0

        lax.fori_loop(0, nk.shape[0] // tile, step, 0)

    @pl.when(zh > 0)
    def _():
        absorb_pair(refs, q_ref, ak[...], av[...])

    @pl.when(zh == 3)
    def _():
        absorb_pair(refs, q_ref, bk[...], bv[...])


def last_kernel(where_ref, q_ref, peak_ref, total_ref, summed_ref, ak, av, bk, bv, *rest):
    outs, own = rest[:4], rest[4:]
    for mine, ref in zip(own, (peak_ref, total_ref, summed_ref)):
        mine[...] = ref[...]

    @pl.when(where_ref[1] > 1)
    def _():
        k = jnp.concatenate([ak[...], bk[...]], 0)
        v = jnp.concatenate([av[...], bv[...]], 0)
        absorb_pair(own, q_ref, k, v)

    for g in range(2):
        result = (own[2][g] / own[1][g]).T.astype(BF)
        for n, out in enumerate(outs):
            out[:, g * HD : (g + 1) * HD] = result[n * 128 : (n + 1) * 128]


def head_specs(rows):
    return [
        pl.BlockSpec((rows, HD), lambda h, w: (0, h)),
        pl.BlockSpec((rows, HD), lambda h, w: (0, 2 + h)),
    ]


def state_shapes(heads, rows):
    return [(heads, 1, rows), (heads, 1, rows), (heads, HD, rows)]


def state_specs(rows):
    return [pl.BlockSpec(shape, lambda h, w: (h, 0, 0)) for shape in state_shapes(2, rows)]


def attention_call(body, name, where, q, state, parts, out_specs, out_shape, scratch, share=1):
    rows = q.shape[0]
    keys = sum(part.shape[0] for part in parts)
    in_specs = [pl.BlockSpec((rows, 2 * HD), lambda h, w: (0, h))]
    if state:
        in_specs += state_specs(rows)
    operands = [q, *state]
    for part in parts:
        in_specs += head_specs(part.shape[0])
        operands += [part, part]
    return pl.pallas_call(
        body,
        grid_spec=pltpu.PrefetchScalarGridSpec(
            num_scalar_prefetch=1,
            grid=(2,),
            in_specs=in_specs,
            out_specs=out_specs,
            scratch_shapes=scratch,
        ),
        out_shape=out_shape,
        compiler_params=pltpu.CompilerParams(vmem_limit_bytes=40 * 1024 * 1024),
        cost_estimate=pl.CostEstimate(
            flops=4 * 4 * rows * keys * HD // share, bytes_accessed=(8 << 20) // share, transcendentals=4 * rows * keys // share
        ),
        name=name,
    )(where, *operands)


def own_part(where, q, own):
    rows = q.shape[0]
    return attention_call(
        own_kernel,
        "own_attention",
        where,
        q,
        (),
        (own,),
        state_specs(rows) + [pl.BlockSpec(memory_space=pltpu.SMEM)],
        [jax.ShapeDtypeStruct(shape, F32) for shape in state_shapes(4, rows)]
        + [jax.ShapeDtypeStruct((3,), jnp.int32)],
        [],
        64,
    )


def middle(where, q, state, parts):
    rows = q.shape[0]
    return attention_call(
        middle_kernel,
        "middle_attention",
        where,
        q,
        state,
        parts,
        state_specs(rows),
        [jax.ShapeDtypeStruct(shape, F32) for shape in state_shapes(4, rows)],
        [],
    )


def last(where, q, state, parts):
    rows = q.shape[0]
    return attention_call(
        last_kernel,
        "last_attention",
        where,
        q,
        state,
        parts,
        [pl.BlockSpec((128, 2 * HD), lambda h, w: (0, h))] * 4,
        [jax.ShapeDtypeStruct((128, 4 * HD), BF)] * 4,
        [pltpu.VMEM(shape, F32) for shape in state_shapes(2, rows)],
    )


def ring(coordinate, step, size):
    return (coordinate + step) % size


def x_shift(step):
    return lambda zl, y, c, zh, x: (zl, y, c, zh, ring(x, step, XX))


def strip_of_anchor(raw, zl, y):
    part = raw.shape[0] // YY
    held = raw[:part]
    for to in range(1, YY):
        got = send(
            raw[to * part : (to + 1) * part],
            lambda zl, y, c, zh, x: (zl, to, c, zh, x) if (zl, y, c) == (0, 0, 0) else None,
        )
        held = jnp.where(y == to, got, held)
    for swap in ((1, 0, 3, 2), (3, 2, 1, 0)):
        got = send(held, lambda zl, y, c, zh, x: (zl, y, c, swap[zh], x) if (zl, c) == (0, 0) else None)
        held = jnp.concatenate([held, got], 0)
    first = lambda zl, c: (zl, c) == (0, 0)
    two = send(held, lambda zl, y, c, zh, x: (2, y, c, zh, x) if first(zl, c) else None)
    one = send(held, lambda zl, y, c, zh, x: (1, y, c, zh, x) if first(zl, c) else None)
    three = send(held, lambda zl, y, c, zh, x: (3, y, c, ring(zh, 3, ZH), x) if first(zl, c) else None)
    return jnp.where(zl == 0, held, jnp.where(zl == 1, one, jnp.where(zl == 2, two, three)))


def gather_y(block):
    half = block.shape[0] // 2
    up = lambda zl, y, c, zh, x: (zl, ring(y, 1, YY), c, zh, x) if c == 0 else None
    down = lambda zl, y, c, zh, x: (zl, ring(y, 3, YY), c, zh, x) if c == 0 else None
    low, high = send(block, up), send(block, down)
    low2, high2 = send(low[:half], up), send(high[half:], down)
    return jnp.concatenate([block, low, high, low2, high2], 0)


def local(queries, keys, values):
    blk = lax.axis_index("blk")
    head = lax.axis_index("head")
    zh, x = head // XX, head % XX
    zl, y, c = blk // (YY * CC), (blk // CC) % YY, blk % CC
    where = jnp.stack([x, zh, blk]).astype(jnp.int32)
    tok = queries.shape[0]

    width = keys.shape[1]
    raw = jnp.concatenate([keys, values], 1)

    def kv_of_head(block, among=lambda c: True):
        def piece(s):
            at = ring(x, s, XX) * 256
            rows = block.shape[0]
            return jnp.concatenate(
                [lax.dynamic_slice(block, (0, start + at), (rows, 256)) for start in (0, width)], 1
            )

        def move(s):
            return lambda zl, y, c, zh, x: (zl, y, c, zh, ring(x, s, XX)) if among(c) else None

        return jnp.concatenate([piece(0)] + [send(piece(s), move(s)) for s in (1, 2, 3)], 0)

    def q_piece(s):
        return lax.dynamic_slice(queries, (0, ring(x, s, XX) * 512), (tok, 512))

    always = blk < 32

    strip, own = lax.cond(
        always,
        lambda: (strip_of_anchor(raw, zl, y), kv_of_head(raw)),
        lambda: (jnp.zeros_like(raw), jnp.zeros((4 * tok, 512), BF)),
    )

    half = own.shape[0] // 2
    got_a = send(own, lambda zl, y, c, zh, x: (zl, y, c, zh + 1, x) if zh < 3 else None)
    got_b = send(own, lambda zl, y, c, zh, x: (zl, y, c, ring(zh, 3, ZH), x) if zh < 2 else None)

    def whole_anchor():
        whole = gather_y(kv_of_head(strip, lambda c: c == 0))
        copied = send(whole, lambda zl, y, c, zh, x: (zl, y, 1, zh, x) if c == 0 else None)
        q = [send(q_piece(s), x_shift(s)) for s in (2, 3)]
        return jnp.where(c == 0, whole, copied), *q, where

    anchor, q2, q3, where = lax.cond(
        always,
        whole_anchor,
        lambda: (jnp.zeros((2048, 512), BF),) + (jnp.zeros((tok, 512), BF),) * 2 + (where - 1,),
    )
    q = jnp.concatenate([q_piece(0), send(q_piece(1), x_shift(1)), q2, q3], 0)

    *state, where = own_part(where, q, own)
    arrived = where[2] >= 0
    got_a2 = send(
        jnp.where(arrived, got_a[:half], own[:half]),
        lambda zl, y, c, zh, x: (zl, y, c, zh + 1, x) if zh in (1, 2) else None,
    )
    got_b2 = send(
        jnp.where(arrived, got_b[half:], own[half:]),
        lambda zl, y, c, zh, x: (zl, y, c, ring(zh, 3, ZH), x) if zh in (0, 3) else None,
    )
    state = middle(where, q, state, (got_a, got_b, anchor))
    pieces = last(where, q, state, (got_a2, got_b2))
    out = jnp.zeros((tok, XX * 512), BF)
    for s in range(XX):
        piece = pieces[s] if s == 0 else send(pieces[s], x_shift(XX - s))
        out = lax.dynamic_update_slice(out, piece, (0, ring(x, s, XX) * 512))
    return out


def solution(mesh):
    spec = P(("blk", "head"), None)
    return jax.shard_map(local, mesh=mesh, in_specs=(spec,) * 3, out_specs=spec, check_vma=False)
```

```python
import functools

import jax
import jax.numpy as jnp
from jax import lax
from jax.experimental import pallas as pl
from jax.experimental.pallas import tpu as pltpu
from jax.sharding import PartitionSpec as P

HD = 128
BF = jnp.bfloat16
F32 = jnp.float32
masked_value = -1e30
exp2_scale = 0.08838834764831845 * 1.4426950408889634

AXES = ("zl", "y", "c", "zh", "x")
SIZES = (4, 4, 2, 4, 4)
HEADS_X = 4


def exchange(block, axes):
    return lax.all_to_all(block, axes, split_axis=0, concat_axis=0, tiled=True)


def gathered(block, axis, size):
    return exchange(jnp.concatenate([block] * size, 0), axis)


def absorb_tile(q, k, v, state, keep=None):
    peak, total, summed = state
    scores = lax.dot_general(k, q, (((1,), (1,)), ((), ())), preferred_element_type=F32)
    if keep is not None:
        scores = jnp.where(keep, scores, masked_value)
    new_peak = jnp.maximum(peak, jnp.max(scores, axis=0, keepdims=True))
    expo = jnp.exp2((scores - new_peak) * exp2_scale)
    rescale = jnp.exp2((peak - new_peak) * exp2_scale)
    total = total * rescale + jnp.sum(expo, axis=0, keepdims=True)
    summed = summed * rescale + lax.dot_general(
        v, expo.astype(BF), (((0,), (0,)), ((), ())), preferred_element_type=F32
    )
    return new_peak, total, summed


def absorb_pair(refs, q_ref, k, v, keep=None, start=None):
    for g in range(2):
        q = q_ref[:, g * HD : (g + 1) * HD]
        state = start or tuple(ref[g] for ref in refs)
        for ref, part in zip(refs, absorb_tile(q, k, v, state, keep)):
            ref[g] = part


def own_kernel(where_ref, q_ref, ok, ov, *outs):
    refs, where_out = outs[:3], outs[3]
    for n in range(3):
        where_out[n] = where_ref[n]
    rows = q_ref.shape[0]

    key_at = lax.broadcasted_iota(jnp.int32, (rows, rows), 0)
    query_at = lax.broadcasted_iota(jnp.int32, (rows, rows), 1)
    start = (
        jnp.full((1, rows), masked_value, F32),
        jnp.zeros((1, rows), F32),
        jnp.zeros((HD, rows), F32),
    )
    absorb_pair(refs, q_ref, ok[...], ov[...], key_at <= query_at, start)


def middle_kernel(where_ref, q_ref, p_ref, t_ref, s_ref, ak, av, bk, bv, nk, nv, mk, mv, *refs):
    zh, blk = where_ref[1], where_ref[2]
    for ref, before in zip(refs, (p_ref, t_ref, s_ref)):
        ref[...] = before[...]

    @pl.when(blk > 0)
    def _():
        tile = 512

        def step(t, _):
            at = pl.ds(pl.multiple_of(t * tile, tile), tile)
            absorb_pair(refs, q_ref, nk[at, :], nv[at, :])
            absorb_pair(refs, q_ref, mk[at, :], mv[at, :])
            return 0

        lax.fori_loop(0, nk.shape[0] // tile, step, 0)

    @pl.when(zh > 0)
    def _():
        absorb_pair(refs, q_ref, ak[...], av[...])

    @pl.when(zh == 3)
    def _():
        absorb_pair(refs, q_ref, bk[...], bv[...])


def last_kernel(where_ref, q_ref, peak_ref, total_ref, summed_ref, ak, av, bk, bv, out_ref, *own):
    for mine, ref in zip(own, (peak_ref, total_ref, summed_ref)):
        mine[...] = ref[...]

    @pl.when(where_ref[1] > 1)
    def _():
        k = jnp.concatenate([ak[...], bk[...]], 0)
        v = jnp.concatenate([av[...], bv[...]], 0)
        absorb_pair(own, q_ref, k, v)

    for g in range(2):
        out_ref[:, g * HD : (g + 1) * HD] = (own[2][g] / own[1][g]).T.astype(BF)


def head_specs(rows):
    return [
        pl.BlockSpec((rows, HD), lambda h, w: (0, h)),
        pl.BlockSpec((rows, HD), lambda h, w: (0, 2 + h)),
    ]


def state_shapes(heads, rows):
    return [(heads, 1, rows), (heads, 1, rows), (heads, HD, rows)]


def state_specs(rows):
    return [pl.BlockSpec(shape, lambda h, w: (h, 0, 0)) for shape in state_shapes(2, rows)]


def attention_call(body, name, where, q, state, parts, out_specs, out_shape, scratch, share=1):
    rows = q.shape[0]
    keys = sum(part.shape[0] for part in parts)
    in_specs = [pl.BlockSpec((rows, 2 * HD), lambda h, w: (0, h))]
    if state:
        in_specs += state_specs(rows)
    operands = [q, *state]
    for part in parts:
        in_specs += head_specs(part.shape[0])
        operands += [part, part]
    return pl.pallas_call(
        body,
        grid_spec=pltpu.PrefetchScalarGridSpec(
            num_scalar_prefetch=1,
            grid=(2,),
            in_specs=in_specs,
            out_specs=out_specs,
            scratch_shapes=scratch,
        ),
        out_shape=out_shape,
        compiler_params=pltpu.CompilerParams(vmem_limit_bytes=40 * 1024 * 1024),
        cost_estimate=pl.CostEstimate(
            flops=4 * 4 * rows * keys * HD // share, bytes_accessed=(8 << 20) // share, transcendentals=4 * rows * keys // share
        ),
        name=name,
    )(where, *operands)


def own_part(where, q, own):
    rows = q.shape[0]
    return attention_call(
        own_kernel,
        "own_attention",
        where,
        q,
        (),
        (own,),
        state_specs(rows) + [pl.BlockSpec(memory_space=pltpu.SMEM)],
        [jax.ShapeDtypeStruct(shape, F32) for shape in state_shapes(4, rows)]
        + [jax.ShapeDtypeStruct((3,), jnp.int32)],
        [],
        64,
    )


def middle(where, q, state, parts):
    rows = q.shape[0]
    return attention_call(
        middle_kernel,
        "middle_attention",
        where,
        q,
        state,
        parts,
        state_specs(rows),
        [jax.ShapeDtypeStruct(shape, F32) for shape in state_shapes(4, rows)],
        [],
    )


def last(where, q, state, parts):
    rows = q.shape[0]
    return attention_call(
        last_kernel,
        "last_attention",
        where,
        q,
        state,
        parts,
        pl.BlockSpec((rows, 2 * HD), lambda h, w: (0, h)),
        jax.ShapeDtypeStruct((rows, 4 * HD), BF),
        [pltpu.VMEM(shape, F32) for shape in state_shapes(2, rows)],
    )


def local(queries, keys, values):
    zl, y, c, zh, x = (lax.axis_index(name) for name in AXES)
    blk = (zl * SIZES[1] + y) * SIZES[2] + c
    where = jnp.stack([x, zh, blk]).astype(jnp.int32)

    own = exchange(
        jnp.concatenate(
            [
                jnp.concatenate([keys[:, n * 256 : (n + 1) * 256], values[:, n * 256 : (n + 1) * 256]], 1)
                for n in range(HEADS_X)
            ],
            0,
        ),
        "x",
    )
    rows = own.shape[0]

    piece = exchange(own, ("zl", "y", "c"))[: rows // 32]
    strip = gathered(gathered(piece, "zh", 4), "zl", 4)

    half = rows // 2
    own, strip = lax.cond(blk < 32, lambda: (own, strip), lambda: (own - own, strip - strip))
    got_a = lax.ppermute(own, "zh", [(0, 1), (1, 2), (2, 3)])
    got_b = lax.ppermute(own, "zh", [(0, 3), (1, 0)])

    def whole_anchor():
        here = gathered(strip, "y", 4)
        return here, lax.ppermute(here, "c", [(0, 1), (1, 0)]), where

    def no_anchor():
        return (jnp.zeros((1024, 512), BF),) * 2 + (where - 1,)

    here, there, where = lax.cond(blk < 32, whole_anchor, no_anchor)
    q = exchange(
        jnp.concatenate([queries[:, n * 512 : (n + 1) * 512] for n in range(HEADS_X)], 0), "x"
    )
    *state, where = own_part(where, q, own)
    arrived = where[2] >= 0
    got_a2 = lax.ppermute(jnp.where(arrived, got_a[:half], own[:half]), "zh", [(1, 2), (2, 3)])
    got_b2 = lax.ppermute(jnp.where(arrived, got_b[half:], own[half:]), "zh", [(3, 2), (0, 3)])
    state = middle(where, q, state, (got_a, got_b, here, there))
    out = exchange(last(where, q, state, (got_a2, got_b2)), "x")
    width = rows // HEADS_X
    return jnp.concatenate([out[n * width : (n + 1) * width] for n in range(HEADS_X)], 1)


def solution(mesh):
    spec = P(AXES, None)
    split = jax.sharding.Mesh(mesh.devices.reshape(SIZES), AXES)
    return jax.shard_map(local, mesh=split, in_specs=(spec,) * 3, out_specs=spec, check_vma=False)
```

```python
import functools

import jax
import jax.numpy as jnp
from jax import lax
from jax.experimental import pallas as pl
from jax.experimental.pallas import tpu as pltpu
from jax.sharding import PartitionSpec as P

HD = 128
BF = jnp.bfloat16
F32 = jnp.float32
masked_value = -1e30
exp2_scale = 0.08838834764831845 * 1.4426950408889634

AXES = ("zl", "y", "c", "zh", "x")
SIZES = (4, 4, 2, 4, 4)
HEADS_X = 4


def exchange(block, axes):
    return lax.all_to_all(block, axes, split_axis=0, concat_axis=0, tiled=True)


def gathered(block, axis, size):
    return exchange(jnp.concatenate([block] * size, 0), axis)


def absorb(refs, q_ref, tiles, causal=False):
    rows = q_ref.shape[0]
    width = rows // 2
    chains = [(g, n) for g in range(2) for n in range(2)]

    def scores_of(chain):
        g, n = chain
        q = q_ref[n * width : (n + 1) * width, g * HD : (g + 1) * HD]
        found = []
        for k, _ in tiles:
            k = k[: (n + 1) * width] if causal else k[...]
            found.append(lax.dot_general(k, q, (((1,), (1,)), ((), ())), preferred_element_type=F32))
        if causal:
            key_at = lax.broadcasted_iota(jnp.int32, found[0].shape, 0)
            query_at = lax.broadcasted_iota(jnp.int32, found[0].shape, 1) + n * width
            found = [jnp.where(key_at <= query_at, found[0], masked_value)]
        return found

    following = scores_of(chains[0])
    for at, (g, n) in enumerate(chains):
        found = following
        if at + 1 < len(chains):
            following = scores_of(chains[at + 1])
        columns = slice(n * width, (n + 1) * width)
        new_peak = functools.reduce(
            jnp.maximum, [jnp.max(scores, axis=0, keepdims=True) for scores in found]
        )
        if not causal:
            peak, total, summed = (ref[g, :, columns] for ref in refs)
            new_peak = jnp.maximum(peak, new_peak)
            rescale = jnp.exp2((peak - new_peak) * exp2_scale)
            new_total, new_summed = total * rescale, summed * rescale
        else:
            new_total, new_summed = 0.0, 0.0
        for scores, (_, v) in zip(found, tiles):
            expo = jnp.exp2((scores - new_peak) * exp2_scale)
            v = v[: (n + 1) * width] if causal else v[...]
            new_total += jnp.sum(expo, axis=0, keepdims=True)
            new_summed += lax.dot_general(
                v, expo.astype(BF), (((0,), (0,)), ((), ())), preferred_element_type=F32
            )
        for ref, part in zip(refs, (new_peak, new_total, new_summed)):
            ref[g, :, columns] = part


def own_kernel(where_ref, q_ref, ok, ov, *outs):
    refs, where_out = outs[:3], outs[3]
    for n in range(3):
        where_out[n] = where_ref[n]
    absorb(refs, q_ref, [(ok, ov)], causal=True)


def middle_kernel(where_ref, q_ref, p_ref, t_ref, s_ref, ak, av, bk, bv, nk, nv, mk, mv, *refs):
    zh, blk = where_ref[1], where_ref[2]
    for ref, before in zip(refs, (p_ref, t_ref, s_ref)):
        ref[...] = before[...]

    @pl.when(blk > 0)
    def _():
        tile = 512

        def step(t, _):
            at = pl.ds(pl.multiple_of(t * tile, tile), tile)
            absorb(refs, q_ref, [(nk[at, :], nv[at, :]), (mk[at, :], mv[at, :])])
            return 0

        lax.fori_loop(0, nk.shape[0] // tile, step, 0)

    @pl.when(jnp.logical_and(zh > 0, zh < 3))
    def _():
        absorb(refs, q_ref, [(ak, av)])

    @pl.when(zh == 3)
    def _():
        absorb(refs, q_ref, [(ak, av), (bk, bv)])


def last_kernel(where_ref, q_ref, peak_ref, total_ref, summed_ref, ak, av, bk, bv, out_ref, *own):
    for mine, ref in zip(own, (peak_ref, total_ref, summed_ref)):
        mine[...] = ref[...]

    @pl.when(where_ref[1] > 1)
    def _():
        absorb(own, q_ref, [(ak, av), (bk, bv)])

    for g in range(2):
        out_ref[:, g * HD : (g + 1) * HD] = (own[2][g] / own[1][g]).T.astype(BF)


def head_specs(rows):
    return [
        pl.BlockSpec((rows, HD), lambda h, w: (0, h)),
        pl.BlockSpec((rows, HD), lambda h, w: (0, 2 + h)),
    ]


def state_shapes(heads, rows):
    return [(heads, 1, rows), (heads, 1, rows), (heads, HD, rows)]


def state_specs(rows):
    return [pl.BlockSpec(shape, lambda h, w: (h, 0, 0)) for shape in state_shapes(2, rows)]


def attention_call(body, name, where, q, state, parts, out_specs, out_shape, scratch, share=1):
    rows = q.shape[0]
    keys = sum(part.shape[0] for part in parts)
    in_specs = [pl.BlockSpec((rows, 2 * HD), lambda h, w: (0, h))]
    if state:
        in_specs += state_specs(rows)
    operands = [q, *state]
    for part in parts:
        in_specs += head_specs(part.shape[0])
        operands += [part, part]
    return pl.pallas_call(
        body,
        grid_spec=pltpu.PrefetchScalarGridSpec(
            num_scalar_prefetch=1,
            grid=(2,),
            in_specs=in_specs,
            out_specs=out_specs,
            scratch_shapes=scratch,
        ),
        out_shape=out_shape,
        compiler_params=pltpu.CompilerParams(vmem_limit_bytes=40 * 1024 * 1024),
        cost_estimate=pl.CostEstimate(
            flops=4 * 4 * rows * keys * HD // share, bytes_accessed=(8 << 20) // share, transcendentals=4 * rows * keys // share
        ),
        name=name,
    )(where, *operands)


def own_part(where, q, own):
    rows = q.shape[0]
    return attention_call(
        own_kernel,
        "own_attention",
        where,
        q,
        (),
        (own,),
        state_specs(rows) + [pl.BlockSpec(memory_space=pltpu.SMEM)],
        [jax.ShapeDtypeStruct(shape, F32) for shape in state_shapes(4, rows)]
        + [jax.ShapeDtypeStruct((3,), jnp.int32)],
        [],
        64,
    )


def middle(where, q, state, parts):
    rows = q.shape[0]
    return attention_call(
        middle_kernel,
        "middle_attention",
        where,
        q,
        state,
        parts,
        state_specs(rows),
        [jax.ShapeDtypeStruct(shape, F32) for shape in state_shapes(4, rows)],
        [],
        10**6,
    )


def last(where, q, state, parts):
    rows = q.shape[0]
    return attention_call(
        last_kernel,
        "last_attention",
        where,
        q,
        state,
        parts,
        pl.BlockSpec((rows, 2 * HD), lambda h, w: (0, h)),
        jax.ShapeDtypeStruct((rows, 4 * HD), BF),
        [pltpu.VMEM(shape, F32) for shape in state_shapes(2, rows)],
    )


def local(queries, keys, values):
    zl, y, c, zh, x = (lax.axis_index(name) for name in AXES)
    blk = (zl * SIZES[1] + y) * SIZES[2] + c
    where = jnp.stack([x, zh, blk]).astype(jnp.int32)

    own = exchange(
        jnp.concatenate(
            [
                jnp.concatenate([keys[:, n * 256 : (n + 1) * 256], values[:, n * 256 : (n + 1) * 256]], 1)
                for n in range(HEADS_X)
            ],
            0,
        ),
        "x",
    )
    rows = own.shape[0]

    half = rows // 2
    got_a = lax.ppermute(own, "zh", [(0, 1), (1, 2), (2, 3)])
    got_b = lax.ppermute(own, "zh", [(0, 3), (1, 0)])

    piece, where = lax.cond(
        blk < 32,
        lambda: (exchange(own, ("zl", "y", "c"))[: rows // 32], where),
        lambda: (jnp.zeros((rows // 32, 512), BF), where - 1),
    )
    q = exchange(
        jnp.concatenate([queries[:, n * 512 : (n + 1) * 512] for n in range(HEADS_X)], 0), "x"
    )
    *state, where = own_part(where, q, own)
    strip, where = lax.cond(
        where[2] < 32,
        lambda: (gathered(piece, ("zl", "zh"), 16), where),
        lambda: (jnp.zeros((rows // 2, 512), BF), where - 1),
    )
    arrived = where[2] >= 0
    got_a2 = lax.ppermute(jnp.where(arrived, got_a[:half], own[:half]), "zh", [(1, 2), (2, 3)])
    got_b2 = lax.ppermute(jnp.where(arrived, got_b[half:], own[half:]), "zh", [(3, 2), (0, 3)])

    def whole_anchor():
        here = gathered(strip, "y", 4)
        return here, lax.ppermute(here, "c", [(0, 1), (1, 0)])

    here, there = lax.cond(blk < 32, whole_anchor, lambda: (jnp.zeros((1024, 512), BF),) * 2)
    state = middle(where, q, state, (got_a, got_b, here, there))
    out = exchange(last(where, q, state, (got_a2, got_b2)), "x")
    width = rows // HEADS_X
    return jnp.concatenate([out[n * width : (n + 1) * width] for n in range(HEADS_X)], 1)


def solution(mesh):
    spec = P(AXES, None)
    split = jax.sharding.Mesh(mesh.devices.reshape(SIZES), AXES)
    return jax.shard_map(local, mesh=split, in_specs=(spec,) * 3, out_specs=spec, check_vma=False)
```

```python
import functools
import itertools

import jax
import jax.numpy as jnp
from jax import lax
from jax.experimental import pallas as pl
from jax.experimental.pallas import tpu as pltpu
from jax.sharding import PartitionSpec as P

HD = 128
BF = jnp.bfloat16
F32 = jnp.float32
masked_value = -1e30
exp2_scale = 0.08838834764831845 * 1.4426950408889634

AXES = ("zl", "y", "c", "zh", "x")
SIZES = (4, 4, 2, 4, 4)
HEADS_X = 4


def exchange(block, axes):
    return lax.all_to_all(block, axes, split_axis=0, concat_axis=0, tiled=True)


def gathered(block, axis, size):
    return exchange(jnp.concatenate([block] * size, 0), axis)


def absorb(refs, q_ref, tiles, causal=False):
    rows = q_ref.shape[0]
    width = rows // 2
    chains = [(g, n) for g in range(2) for n in range(2)]

    def scores_of(chain):
        g, n = chain
        q = q_ref[n * width : (n + 1) * width, g * HD : (g + 1) * HD]
        found = []
        for k, _ in tiles:
            k = k[: (n + 1) * width] if causal else k[...]
            found.append(lax.dot_general(k, q, (((1,), (1,)), ((), ())), preferred_element_type=F32))
        if causal:
            key_at = lax.broadcasted_iota(jnp.int32, found[0].shape, 0)
            query_at = lax.broadcasted_iota(jnp.int32, found[0].shape, 1) + n * width
            found = [jnp.where(key_at <= query_at, found[0], masked_value)]
        return found

    following = scores_of(chains[0])
    for at, (g, n) in enumerate(chains):
        found = following
        if at + 1 < len(chains):
            following = scores_of(chains[at + 1])
        columns = slice(n * width, (n + 1) * width)
        new_peak = functools.reduce(
            jnp.maximum, [jnp.max(scores, axis=0, keepdims=True) for scores in found]
        )
        if not causal:
            peak, total, summed = (ref[g, :, columns] for ref in refs)
            new_peak = jnp.maximum(peak, new_peak)
            rescale = jnp.exp2((peak - new_peak) * exp2_scale)
            new_total, new_summed = total * rescale, summed * rescale
        else:
            new_total, new_summed = 0.0, 0.0
        for scores, (_, v) in zip(found, tiles):
            expo = jnp.exp2((scores - new_peak) * exp2_scale)
            v = v[: (n + 1) * width] if causal else v[...]
            new_total += jnp.sum(expo, axis=0, keepdims=True)
            new_summed += lax.dot_general(
                v, expo.astype(BF), (((0,), (0,)), ((), ())), preferred_element_type=F32
            )
        for ref, part in zip(refs, (new_peak, new_total, new_summed)):
            ref[g, :, columns] = part


def own_kernel(where_ref, q_ref, ok, ov, *refs):
    absorb(refs, q_ref, [(ok, ov)], causal=True)


def middle_kernel(where_ref, q_ref, p_ref, t_ref, s_ref, ak, av, bk, bv, nk, nv, mk, mv, *refs):
    zh, blk = where_ref[1], where_ref[2]
    for ref, before in zip(refs, (p_ref, t_ref, s_ref)):
        ref[...] = before[...]

    @pl.when(blk > 0)
    def _():
        tile = 512

        def step(t, _):
            at = pl.ds(pl.multiple_of(t * tile, tile), tile)
            absorb(refs, q_ref, [(nk[at, :], nv[at, :]), (mk[at, :], mv[at, :])])
            return 0

        lax.fori_loop(0, nk.shape[0] // tile, step, 0)

    @pl.when(jnp.logical_and(zh > 0, zh < 3))
    def _():
        absorb(refs, q_ref, [(ak, av)])

    @pl.when(zh == 3)
    def _():
        absorb(refs, q_ref, [(ak, av), (bk, bv)])


def last_kernel(where_ref, q_ref, peak_ref, total_ref, summed_ref, ak, av, bk, bv, out_ref, *own):
    for mine, ref in zip(own, (peak_ref, total_ref, summed_ref)):
        mine[...] = ref[...]

    @pl.when(where_ref[1] > 1)
    def _():
        absorb(own, q_ref, [(ak, av), (bk, bv)])

    for g in range(2):
        out_ref[:, g * HD : (g + 1) * HD] = (own[2][g] / own[1][g]).T.astype(BF)


def head_specs(rows):
    return [
        pl.BlockSpec((rows, HD), lambda h, w: (0, h)),
        pl.BlockSpec((rows, HD), lambda h, w: (0, 2 + h)),
    ]


def state_shapes(heads, rows):
    return [(heads, 1, rows), (heads, 1, rows), (heads, HD, rows)]


def state_specs(rows):
    return [pl.BlockSpec(shape, lambda h, w: (h, 0, 0)) for shape in state_shapes(2, rows)]


def attention_call(body, name, where, q, state, parts, out_specs, out_shape, scratch, share=1):
    rows = q.shape[0]
    keys = sum(part.shape[0] for part in parts)
    in_specs = [pl.BlockSpec((rows, 2 * HD), lambda h, w: (0, h))]
    if state:
        in_specs += state_specs(rows)
    operands = [q, *state]
    for part in parts:
        in_specs += head_specs(part.shape[0])
        operands += [part, part]
    return pl.pallas_call(
        body,
        grid_spec=pltpu.PrefetchScalarGridSpec(
            num_scalar_prefetch=1,
            grid=(2,),
            in_specs=in_specs,
            out_specs=out_specs,
            scratch_shapes=scratch,
        ),
        out_shape=out_shape,
        compiler_params=pltpu.CompilerParams(vmem_limit_bytes=40 * 1024 * 1024),
        cost_estimate=pl.CostEstimate(
            flops=4 * 4 * rows * keys * HD // share, bytes_accessed=(8 << 20) // share, transcendentals=4 * rows * keys // share
        ),
        name=name,
    )(where, *operands)


def own_part(where, q, own):
    rows = q.shape[0]
    return attention_call(
        own_kernel,
        "own_attention",
        where,
        q,
        (),
        (own,),
        state_specs(rows),
        [jax.ShapeDtypeStruct(shape, F32) for shape in state_shapes(4, rows)],
        [],
        64,
    )


def middle(where, q, state, parts):
    rows = q.shape[0]
    return attention_call(
        middle_kernel,
        "middle_attention",
        where,
        q,
        state,
        parts,
        state_specs(rows),
        [jax.ShapeDtypeStruct(shape, F32) for shape in state_shapes(4, rows)],
        [],
        10**6,
    )


def last(where, q, state, parts):
    rows = q.shape[0]
    return attention_call(
        last_kernel,
        "last_attention",
        where,
        q,
        state,
        parts,
        pl.BlockSpec((rows, 2 * HD), lambda h, w: (0, h)),
        jax.ShapeDtypeStruct((rows, 4 * HD), BF),
        [pltpu.VMEM(shape, F32) for shape in state_shapes(2, rows)],
    )


def device_index(zl, y, c, zh, x):
    return (((zl * 4 + y) * 2 + c) * 4 + zh) * 4 + x


def send(block, move):
    places = itertools.product(*(range(size) for size in SIZES))
    moves = [(place, move(*place)) for place in places]
    return lax.ppermute(
        block, AXES, [(device_index(*place), device_index(*to)) for place, to in moves if to is not None]
    )


def of_heads(block):
    width = block.shape[1] // 2
    return jnp.concatenate(
        [
            jnp.concatenate(
                [block[:, n * 256 : (n + 1) * 256], block[:, width + n * 256 : width + (n + 1) * 256]], 1
            )
            for n in range(HEADS_X)
        ],
        0,
    )


def local(queries, keys, values):
    zl, y, c, zh, x = (lax.axis_index(name) for name in AXES)
    blk = (zl * SIZES[1] + y) * SIZES[2] + c
    where = jnp.stack([x, zh, blk]).astype(jnp.int32)
    always = blk < 32
    raw = jnp.concatenate([keys, values], 1)

    own = exchange(of_heads(raw), "x")
    rows = own.shape[0]
    quarter = rows // 4

    def onward(n):
        part = own[n * quarter : (n + 1) * quarter]
        return (
            lax.ppermute(part, "zh", [(0, 1), (1, 2), (2, 3)]),
            lax.ppermute(part, "zh", [(0, 3), (1, 0)]),
        )

    def step(body, *operands):
        shapes = jax.eval_shape(body, *operands)
        return lax.cond(
            always,
            body,
            lambda *_: jax.tree.map(lambda one: jnp.zeros(one.shape, one.dtype), shapes),
            *operands,
        )

    part = raw.shape[0] // 4
    held = raw[:part]
    for to in range(1, 4):
        got = send(
            raw[to * part : (to + 1) * part],
            lambda zl, y, c, zh, x: (0, to, 0, zh, x) if (zl, y, c) == (0, 0, 0) else None,
        )
        held = jnp.where(y == to, got, held)

    def doubled(held, swap):
        got = send(held, lambda zl, y, c, zh, x: (0, y, 0, swap[zh], x) if (zl, c) == (0, 0) else None)
        return jnp.concatenate([held, got], 0)

    held, *kv0 = step(lambda held: (doubled(held, (1, 0, 3, 2)), *onward(0)), held)

    def second(held):
        q = exchange(
            jnp.concatenate([queries[:, n * 512 : (n + 1) * 512] for n in range(HEADS_X)], 0), "x"
        )
        return (doubled(held, (3, 2, 1, 0)), q, *onward(1))

    held, q, *kv1 = step(second, held)

    def third(held):
        first = lambda zl, c: (zl, c) == (0, 0)
        two = send(held, lambda zl, y, c, zh, x: (2, y, 0, zh, x) if first(zl, c) else None)
        one = send(held, lambda zl, y, c, zh, x: (1, y, 0, zh, x) if first(zl, c) else None)
        three = send(held, lambda zl, y, c, zh, x: (3, y, 0, (zh + 3) % 4, x) if first(zl, c) else None)
        strip = jnp.where(zl == 0, held, jnp.where(zl == 1, one, jnp.where(zl == 2, two, three)))
        half = strip.shape[0] // 2
        moved = lax.ppermute(strip[half:], "c", [(0, 1)])
        return (jnp.where(c == 0, strip[:half], moved), *onward(2))

    strip, *kv2 = step(third, held)
    strip, *kv3 = step(lambda strip: (exchange(of_heads(strip), "x"), *onward(3)), strip)

    got_a, got_b = (jnp.concatenate(parts, 0) for parts in zip(kv0, kv1, kv2, kv3))
    half = rows // 2
    got_a2 = lax.ppermute(got_a[:half], "zh", [(1, 2), (2, 3)])
    got_b2 = lax.ppermute(got_b[half:], "zh", [(3, 2), (0, 3)])

    def whole_anchor(strip):
        here = gathered(strip, "y", 4)
        return here, lax.ppermute(here, "c", [(0, 1), (1, 0)]), *own_part(where, q, own)

    here, there, *state = step(whole_anchor, strip)
    state = middle(where, q, state, (got_a, got_b, here, there))
    out = exchange(last(where, q, state, (got_a2, got_b2)), "x")
    width = rows // HEADS_X
    return jnp.concatenate([out[n * width : (n + 1) * width] for n in range(HEADS_X)], 1)


def solution(mesh):
    spec = P(AXES, None)
    split = jax.sharding.Mesh(mesh.devices.reshape(SIZES), AXES)
    return jax.shard_map(local, mesh=split, in_specs=(spec,) * 3, out_specs=spec, check_vma=False)
```

```python
import functools
import itertools

import jax
import jax.numpy as jnp
from jax import lax
from jax.experimental import pallas as pl
from jax.experimental.pallas import tpu as pltpu
from jax.sharding import PartitionSpec as P

HD = 128
BF = jnp.bfloat16
F32 = jnp.float32
masked_value = -1e30
exp2_scale = 0.08838834764831845 * 1.4426950408889634

AXES = ("zl", "y", "c", "zh", "x")
SIZES = (4, 4, 2, 4, 4)
HEADS_X = 4


def exchange(block, axes):
    return lax.all_to_all(block, axes, split_axis=0, concat_axis=0, tiled=True)


def gathered(block, axis, size):
    return exchange(jnp.concatenate([block] * size, 0), axis)


def absorb(refs, q_ref, tiles, causal=False):
    rows = q_ref.shape[0]
    width = rows // 2
    chains = [(g, n) for g in range(2) for n in range(2)]

    def scores_of(chain):
        g, n = chain
        q = q_ref[n * width : (n + 1) * width, g * HD : (g + 1) * HD]
        found = []
        for k, _ in tiles:
            k = k[: (n + 1) * width] if causal else k[...]
            found.append(lax.dot_general(k, q, (((1,), (1,)), ((), ())), preferred_element_type=F32))
        if causal:
            key_at = lax.broadcasted_iota(jnp.int32, found[0].shape, 0)
            query_at = lax.broadcasted_iota(jnp.int32, found[0].shape, 1) + n * width
            found = [jnp.where(key_at <= query_at, found[0], masked_value)]
        return found

    following = scores_of(chains[0])
    for at, (g, n) in enumerate(chains):
        found = following
        if at + 1 < len(chains):
            following = scores_of(chains[at + 1])
        columns = slice(n * width, (n + 1) * width)
        new_peak = functools.reduce(
            jnp.maximum, [jnp.max(scores, axis=0, keepdims=True) for scores in found]
        )
        if not causal:
            peak, total, summed = (ref[g, :, columns] for ref in refs)
            new_peak = jnp.maximum(peak, new_peak)
            rescale = jnp.exp2((peak - new_peak) * exp2_scale)
            new_total, new_summed = total * rescale, summed * rescale
        else:
            new_total, new_summed = 0.0, 0.0
        for scores, (_, v) in zip(found, tiles):
            expo = jnp.exp2((scores - new_peak) * exp2_scale)
            v = v[: (n + 1) * width] if causal else v[...]
            new_total += jnp.sum(expo, axis=0, keepdims=True)
            new_summed += lax.dot_general(
                v, expo.astype(BF), (((0,), (0,)), ((), ())), preferred_element_type=F32
            )
        for ref, part in zip(refs, (new_peak, new_total, new_summed)):
            ref[g, :, columns] = part


def own_kernel(where_ref, q_ref, ok, ov, *outs):
    refs, where_out = outs[:3], outs[3]
    for n in range(3):
        where_out[n] = where_ref[n]
    absorb(refs, q_ref, [(ok, ov)], causal=True)


def middle_kernel(where_ref, q_ref, p_ref, t_ref, s_ref, ak, av, bk, bv, nk, nv, mk, mv, *refs):
    zh, blk = where_ref[1], where_ref[2]
    for ref, before in zip(refs, (p_ref, t_ref, s_ref)):
        ref[...] = before[...]

    @pl.when(blk > 0)
    def _():
        tile = 512

        def step(t, _):
            at = pl.ds(pl.multiple_of(t * tile, tile), tile)
            absorb(refs, q_ref, [(nk[at, :], nv[at, :]), (mk[at, :], mv[at, :])])
            return 0

        lax.fori_loop(0, nk.shape[0] // tile, step, 0)

    @pl.when(jnp.logical_and(zh > 0, zh < 3))
    def _():
        absorb(refs, q_ref, [(ak, av)])

    @pl.when(zh == 3)
    def _():
        absorb(refs, q_ref, [(ak, av), (bk, bv)])


def last_kernel(where_ref, q_ref, peak_ref, total_ref, summed_ref, ak, av, bk, bv, out_ref, *own):
    for mine, ref in zip(own, (peak_ref, total_ref, summed_ref)):
        mine[...] = ref[...]

    @pl.when(where_ref[1] > 1)
    def _():
        absorb(own, q_ref, [(ak, av), (bk, bv)])

    for g in range(2):
        out_ref[:, g * HD : (g + 1) * HD] = (own[2][g] / own[1][g]).T.astype(BF)


def head_specs(rows):
    return [
        pl.BlockSpec((rows, HD), lambda h, w: (0, h)),
        pl.BlockSpec((rows, HD), lambda h, w: (0, 2 + h)),
    ]


def state_shapes(heads, rows):
    return [(heads, 1, rows), (heads, 1, rows), (heads, HD, rows)]


def state_specs(rows):
    return [pl.BlockSpec(shape, lambda h, w: (h, 0, 0)) for shape in state_shapes(2, rows)]


def attention_call(body, name, where, q, state, parts, out_specs, out_shape, scratch, share=1):
    rows = q.shape[0]
    keys = sum(part.shape[0] for part in parts)
    in_specs = [pl.BlockSpec((rows, 2 * HD), lambda h, w: (0, h))]
    if state:
        in_specs += state_specs(rows)
    operands = [q, *state]
    for part in parts:
        in_specs += head_specs(part.shape[0])
        operands += [part, part]
    return pl.pallas_call(
        body,
        grid_spec=pltpu.PrefetchScalarGridSpec(
            num_scalar_prefetch=1,
            grid=(2,),
            in_specs=in_specs,
            out_specs=out_specs,
            scratch_shapes=scratch,
        ),
        out_shape=out_shape,
        compiler_params=pltpu.CompilerParams(vmem_limit_bytes=40 * 1024 * 1024),
        cost_estimate=pl.CostEstimate(
            flops=4 * 4 * rows * keys * HD // share, bytes_accessed=(8 << 20) // share, transcendentals=4 * rows * keys // share
        ),
        name=name,
    )(where, *operands)


def own_part(where, q, own):
    rows = q.shape[0]
    return attention_call(
        own_kernel,
        "own_attention",
        where,
        q,
        (),
        (own,),
        state_specs(rows) + [pl.BlockSpec(memory_space=pltpu.SMEM)],
        [jax.ShapeDtypeStruct(shape, F32) for shape in state_shapes(4, rows)]
        + [jax.ShapeDtypeStruct((3,), jnp.int32)],
        [],
        64,
    )


def middle(where, q, state, parts):
    rows = q.shape[0]
    return attention_call(
        middle_kernel,
        "middle_attention",
        where,
        q,
        state,
        parts,
        state_specs(rows),
        [jax.ShapeDtypeStruct(shape, F32) for shape in state_shapes(4, rows)],
        [],
    )


def last(where, q, state, parts):
    rows = q.shape[0]
    return attention_call(
        last_kernel,
        "last_attention",
        where,
        q,
        state,
        parts,
        pl.BlockSpec((rows, 2 * HD), lambda h, w: (0, h)),
        jax.ShapeDtypeStruct((rows, 4 * HD), BF),
        [pltpu.VMEM(shape, F32) for shape in state_shapes(2, rows)],
    )


def device_index(zl, y, c, zh, x):
    return (((zl * 4 + y) * 2 + c) * 4 + zh) * 4 + x


def send(block, move):
    places = itertools.product(*(range(size) for size in SIZES))
    moves = [(place, move(*place)) for place in places]
    return lax.ppermute(
        block, AXES, [(device_index(*place), device_index(*to)) for place, to in moves if to is not None]
    )


def of_heads(block):
    width = block.shape[1] // 2
    return jnp.concatenate(
        [
            jnp.concatenate(
                [block[:, n * 256 : (n + 1) * 256], block[:, width + n * 256 : width + (n + 1) * 256]], 1
            )
            for n in range(HEADS_X)
        ],
        0,
    )


def local(queries, keys, values):
    zl, y, c, zh, x = (lax.axis_index(name) for name in AXES)
    blk = (zl * SIZES[1] + y) * SIZES[2] + c
    where = jnp.stack([x, zh, blk]).astype(jnp.int32)
    always = blk < 32
    raw = jnp.concatenate([keys, values], 1)

    own = exchange(of_heads(raw), "x")
    rows = own.shape[0]
    def step(body, *operands):
        shapes = jax.eval_shape(body, *operands)
        return lax.cond(
            always,
            body,
            lambda *_: jax.tree.map(lambda one: jnp.zeros(one.shape, one.dtype), shapes),
            *operands,
        )

    part = raw.shape[0] // 4
    held = raw[:part]
    for to in range(1, 4):
        got = send(
            raw[to * part : (to + 1) * part],
            lambda zl, y, c, zh, x: (0, to, 0, zh, x) if (zl, y, c) == (0, 0, 0) else None,
        )
        held = jnp.where(y == to, got, held)

    def doubled(held, swap):
        got = send(held, lambda zl, y, c, zh, x: (0, y, 0, swap[zh], x) if (zl, c) == (0, 0) else None)
        return jnp.concatenate([held, got], 0)

    def over_z(held, own):
        held = doubled(doubled(held, (1, 0, 3, 2)), (3, 2, 1, 0))
        first = lambda zl, c: (zl, c) == (0, 0)
        two = send(held, lambda zl, y, c, zh, x: (2, y, 0, zh, x) if first(zl, c) else None)
        one = send(held, lambda zl, y, c, zh, x: (1, y, 0, zh, x) if first(zl, c) else None)
        three = send(held, lambda zl, y, c, zh, x: (3, y, 0, (zh + 3) % 4, x) if first(zl, c) else None)
        strip = jnp.where(zl == 0, held, jnp.where(zl == 1, one, jnp.where(zl == 2, two, three)))
        half = strip.shape[0] // 2
        moved = lax.ppermute(strip[half:], "c", [(0, 1)])
        return jnp.where(c == 0, strip[:half], moved), own

    strip, own = step(over_z, held, own)

    half = rows // 2
    got_b = lax.ppermute(own, "zh", [(0, 3), (1, 0)])
    got_a = lax.ppermute(own, "zh", [(0, 1), (1, 2), (2, 3)])

    def whole_anchor(strip, where):
        here = gathered(exchange(of_heads(strip), "x"), "y", 4)
        return here, lax.ppermute(here, "c", [(0, 1), (1, 0)]), where

    here, there, where = step(whole_anchor, strip, where)
    q = exchange(
        jnp.concatenate([queries[:, n * 512 : (n + 1) * 512] for n in range(HEADS_X)], 0), "x"
    )
    *state, where = own_part(where, q, own)
    arrived = where[2] >= 0
    got_a2 = lax.ppermute(jnp.where(arrived, got_a[:half], own[:half]), "zh", [(1, 2), (2, 3)])
    got_b2 = lax.ppermute(jnp.where(arrived, got_b[half:], own[half:]), "zh", [(3, 2), (0, 3)])
    state = middle(where, q, state, (got_a, got_b, here, there))
    out = exchange(last(where, q, state, (got_a2, got_b2)), "x")
    width = rows // HEADS_X
    return jnp.concatenate([out[n * width : (n + 1) * width] for n in range(HEADS_X)], 1)


def solution(mesh):
    spec = P(AXES, None)
    split = jax.sharding.Mesh(mesh.devices.reshape(SIZES), AXES)
    return jax.shard_map(local, mesh=split, in_specs=(spec,) * 3, out_specs=spec, check_vma=False)
```

```python
import functools
import itertools

import jax
import jax.numpy as jnp
from jax import lax
from jax.experimental import pallas as pl
from jax.experimental.pallas import tpu as pltpu
from jax.sharding import PartitionSpec as P

HD = 128
BF = jnp.bfloat16
F32 = jnp.float32
masked_value = -1e30
exp2_scale = 0.08838834764831845 * 1.4426950408889634

AXES = ("zl", "y", "c", "zh", "x")
SIZES = (4, 4, 2, 4, 4)
HEADS_X = 4


def exchange(block, axes):
    return lax.all_to_all(block, axes, split_axis=0, concat_axis=0, tiled=True)


def gathered(block, axis, size):
    return exchange(jnp.concatenate([block] * size, 0), axis)


def absorb(refs, q_ref, tiles, causal=False):
    rows = q_ref.shape[0]
    width = rows // 2
    chains = [(g, n) for g in range(2) for n in range(2)]

    def scores_of(chain):
        g, n = chain
        q = q_ref[n * width : (n + 1) * width, g * HD : (g + 1) * HD]
        found = []
        for k, _ in tiles:
            k = k[: (n + 1) * width] if causal else k[...]
            found.append(lax.dot_general(k, q, (((1,), (1,)), ((), ())), preferred_element_type=F32))
        if causal:
            key_at = lax.broadcasted_iota(jnp.int32, found[0].shape, 0)
            query_at = lax.broadcasted_iota(jnp.int32, found[0].shape, 1) + n * width
            found = [jnp.where(key_at <= query_at, found[0], masked_value)]
        return found

    following = scores_of(chains[0])
    for at, (g, n) in enumerate(chains):
        found = following
        if at + 1 < len(chains):
            following = scores_of(chains[at + 1])
        columns = slice(n * width, (n + 1) * width)
        new_peak = functools.reduce(
            jnp.maximum, [jnp.max(scores, axis=0, keepdims=True) for scores in found]
        )
        if not causal:
            peak, total, summed = (ref[g, :, columns] for ref in refs)
            new_peak = jnp.maximum(peak, new_peak)
            rescale = jnp.exp2((peak - new_peak) * exp2_scale)
            new_total, new_summed = total * rescale, summed * rescale
        else:
            new_total, new_summed = 0.0, 0.0
        for scores, (_, v) in zip(found, tiles):
            expo = jnp.exp2((scores - new_peak) * exp2_scale)
            v = v[: (n + 1) * width] if causal else v[...]
            new_total += jnp.sum(expo, axis=0, keepdims=True)
            new_summed += lax.dot_general(
                v, expo.astype(BF), (((0,), (0,)), ((), ())), preferred_element_type=F32
            )
        for ref, part in zip(refs, (new_peak, new_total, new_summed)):
            ref[g, :, columns] = part


def own_kernel(where_ref, q_ref, ok, ov, *outs):
    refs, where_out = outs[:3], outs[3]
    for n in range(3):
        where_out[n] = where_ref[n]
    absorb(refs, q_ref, [(ok, ov)], causal=True)


def middle_kernel(where_ref, q_ref, p_ref, t_ref, s_ref, ak, av, bk, bv, nk, nv, mk, mv, *refs):
    zh, blk = where_ref[1], where_ref[2]
    for ref, before in zip(refs, (p_ref, t_ref, s_ref)):
        ref[...] = before[...]

    @pl.when(blk > 0)
    def _():
        tile = 512

        def step(t, _):
            at = pl.ds(pl.multiple_of(t * tile, tile), tile)
            absorb(refs, q_ref, [(nk[at, :], nv[at, :]), (mk[at, :], mv[at, :])])
            return 0

        lax.fori_loop(0, nk.shape[0] // tile, step, 0)

    @pl.when(jnp.logical_and(zh > 0, zh < 3))
    def _():
        absorb(refs, q_ref, [(ak, av)])

    @pl.when(zh == 3)
    def _():
        absorb(refs, q_ref, [(ak, av), (bk, bv)])


def last_kernel(where_ref, q_ref, peak_ref, total_ref, summed_ref, ak, av, bk, bv, out_ref, *own):
    for mine, ref in zip(own, (peak_ref, total_ref, summed_ref)):
        mine[...] = ref[...]

    @pl.when(where_ref[1] > 1)
    def _():
        absorb(own, q_ref, [(ak, av), (bk, bv)])

    for g in range(2):
        out_ref[:, g * HD : (g + 1) * HD] = (own[2][g] / own[1][g]).T.astype(BF)


def head_specs(rows):
    return [
        pl.BlockSpec((rows, HD), lambda h, w: (0, h)),
        pl.BlockSpec((rows, HD), lambda h, w: (0, 2 + h)),
    ]


def state_shapes(heads, rows):
    return [(heads, 1, rows), (heads, 1, rows), (heads, HD, rows)]


def state_specs(rows):
    return [pl.BlockSpec(shape, lambda h, w: (h, 0, 0)) for shape in state_shapes(2, rows)]


def attention_call(body, name, where, q, state, parts, out_specs, out_shape, scratch, share=1):
    rows = q.shape[0]
    keys = sum(part.shape[0] for part in parts)
    in_specs = [pl.BlockSpec((rows, 2 * HD), lambda h, w: (0, h))]
    if state:
        in_specs += state_specs(rows)
    operands = [q, *state]
    for part in parts:
        in_specs += head_specs(part.shape[0])
        operands += [part, part]
    return pl.pallas_call(
        body,
        grid_spec=pltpu.PrefetchScalarGridSpec(
            num_scalar_prefetch=1,
            grid=(2,),
            in_specs=in_specs,
            out_specs=out_specs,
            scratch_shapes=scratch,
        ),
        out_shape=out_shape,
        compiler_params=pltpu.CompilerParams(vmem_limit_bytes=40 * 1024 * 1024),
        cost_estimate=pl.CostEstimate(
            flops=4 * 4 * rows * keys * HD // share, bytes_accessed=(8 << 20) // share, transcendentals=4 * rows * keys // share
        ),
        name=name,
    )(where, *operands)


def own_part(where, q, own):
    rows = q.shape[0]
    return attention_call(
        own_kernel,
        "own_attention",
        where,
        q,
        (),
        (own,),
        state_specs(rows) + [pl.BlockSpec(memory_space=pltpu.SMEM)],
        [jax.ShapeDtypeStruct(shape, F32) for shape in state_shapes(4, rows)]
        + [jax.ShapeDtypeStruct((3,), jnp.int32)],
        [],
        64,
    )


def middle(where, q, state, parts):
    rows = q.shape[0]
    return attention_call(
        middle_kernel,
        "middle_attention",
        where,
        q,
        state,
        parts,
        state_specs(rows),
        [jax.ShapeDtypeStruct(shape, F32) for shape in state_shapes(4, rows)],
        [],
    )


def last(where, q, state, parts):
    rows = q.shape[0]
    return attention_call(
        last_kernel,
        "last_attention",
        where,
        q,
        state,
        parts,
        pl.BlockSpec((rows, 2 * HD), lambda h, w: (0, h)),
        jax.ShapeDtypeStruct((rows, 4 * HD), BF),
        [pltpu.VMEM(shape, F32) for shape in state_shapes(2, rows)],
    )


def device_index(zl, y, c, zh, x):
    return (((zl * 4 + y) * 2 + c) * 4 + zh) * 4 + x


def send(block, move):
    places = itertools.product(*(range(size) for size in SIZES))
    moves = [(place, move(*place)) for place in places]
    return lax.ppermute(
        block, AXES, [(device_index(*place), device_index(*to)) for place, to in moves if to is not None]
    )


def of_heads(block):
    width = block.shape[1] // 2
    return jnp.concatenate(
        [
            jnp.concatenate(
                [block[:, n * 256 : (n + 1) * 256], block[:, width + n * 256 : width + (n + 1) * 256]], 1
            )
            for n in range(HEADS_X)
        ],
        0,
    )


def local(queries, keys, values):
    zl, y, c, zh, x = (lax.axis_index(name) for name in AXES)
    blk = (zl * SIZES[1] + y) * SIZES[2] + c
    where = jnp.stack([x, zh, blk]).astype(jnp.int32)
    always = blk < 32
    raw = jnp.concatenate([keys, values], 1)

    own = exchange(of_heads(raw), "x")
    rows = own.shape[0]
    def step(body, *operands):
        shapes = jax.eval_shape(body, *operands)
        return lax.cond(
            always,
            body,
            lambda *_: jax.tree.map(lambda one: jnp.zeros(one.shape, one.dtype), shapes),
            *operands,
        )

    part = raw.shape[0] // 4
    held = raw[:part]
    for to in range(1, 4):
        got = send(
            raw[to * part : (to + 1) * part],
            lambda zl, y, c, zh, x: (0, to, 0, zh, x) if (zl, y, c) == (0, 0, 0) else None,
        )
        held = jnp.where(y == to, got, held)

    def doubled(held, swap):
        got = send(held, lambda zl, y, c, zh, x: (0, y, 0, swap[zh], x) if (zl, c) == (0, 0) else None)
        return jnp.concatenate([held, got], 0)

    def pair_and_queries(held):
        q = exchange(
            jnp.concatenate([queries[:, n * 512 : (n + 1) * 512] for n in range(HEADS_X)], 0), "x"
        )
        return doubled(held, (1, 0, 3, 2)), q

    def over_z(held, own):
        held = doubled(held, (3, 2, 1, 0))
        first = lambda zl, c: (zl, c) == (0, 0)
        two = send(held, lambda zl, y, c, zh, x: (2, y, 0, zh, x) if first(zl, c) else None)
        one = send(held, lambda zl, y, c, zh, x: (1, y, 0, zh, x) if first(zl, c) else None)
        three = send(held, lambda zl, y, c, zh, x: (3, y, 0, (zh + 3) % 4, x) if first(zl, c) else None)
        strip = jnp.where(zl == 0, held, jnp.where(zl == 1, one, jnp.where(zl == 2, two, three)))
        half = strip.shape[0] // 2
        moved = lax.ppermute(strip[half:], "c", [(0, 1)])
        return jnp.where(c == 0, strip[:half], moved), own

    held, q = step(pair_and_queries, held)
    strip, own = step(over_z, held, own)

    half = rows // 2
    got_b = lax.ppermute(own, "zh", [(0, 3), (1, 0)])
    got_a = lax.ppermute(own, "zh", [(0, 1), (1, 2), (2, 3)])

    def whole_anchor(strip, where):
        here = gathered(exchange(of_heads(strip), "x"), "y", 4)
        return here, lax.ppermute(here, "c", [(0, 1), (1, 0)]), where

    here, there, where = step(whole_anchor, strip, where)
    *state, where = own_part(where, q, own)
    arrived = where[2] >= 0
    got_a2 = lax.ppermute(jnp.where(arrived, got_a[:half], own[:half]), "zh", [(1, 2), (2, 3)])
    got_b2 = lax.ppermute(jnp.where(arrived, got_b[half:], own[half:]), "zh", [(3, 2), (0, 3)])
    state = middle(where, q, state, (got_a, got_b, here, there))
    out = exchange(last(where, q, state, (got_a2, got_b2)), "x")
    width = rows // HEADS_X
    return jnp.concatenate([out[n * width : (n + 1) * width] for n in range(HEADS_X)], 1)


def solution(mesh):
    spec = P(AXES, None)
    split = jax.sharding.Mesh(mesh.devices.reshape(SIZES), AXES)
    return jax.shard_map(local, mesh=split, in_specs=(spec,) * 3, out_specs=spec, check_vma=False)
```

```python
import functools
import itertools

import jax
import jax.numpy as jnp
from jax import lax
from jax.experimental import pallas as pl
from jax.experimental.pallas import tpu as pltpu
from jax.sharding import PartitionSpec as P

HD = 128
BF = jnp.bfloat16
F32 = jnp.float32
masked_value = -1e30
exp2_scale = 0.08838834764831845 * 1.4426950408889634

AXES = ("zl", "y", "c", "zh", "x")
SIZES = (4, 4, 2, 4, 4)
HEADS_X = 4


def exchange(block, axes):
    return lax.all_to_all(block, axes, split_axis=0, concat_axis=0, tiled=True)


def gathered(block, axis, size):
    return exchange(jnp.concatenate([block] * size, 0), axis)


def absorb(refs, q_ref, tiles, causal=False):
    rows = q_ref.shape[0]
    width = rows // 2
    chains = [(g, n) for g in range(2) for n in range(2)]

    def scores_of(chain):
        g, n = chain
        q = q_ref[n * width : (n + 1) * width, g * HD : (g + 1) * HD]
        found = []
        for k, _ in tiles:
            k = k[: (n + 1) * width] if causal else k[...]
            found.append(lax.dot_general(k, q, (((1,), (1,)), ((), ())), preferred_element_type=F32))
        if causal:
            key_at = lax.broadcasted_iota(jnp.int32, found[0].shape, 0)
            query_at = lax.broadcasted_iota(jnp.int32, found[0].shape, 1) + n * width
            found = [jnp.where(key_at <= query_at, found[0], masked_value)]
        return found

    following = scores_of(chains[0])
    for at, (g, n) in enumerate(chains):
        found = following
        if at + 1 < len(chains):
            following = scores_of(chains[at + 1])
        columns = slice(n * width, (n + 1) * width)
        new_peak = functools.reduce(
            jnp.maximum, [jnp.max(scores, axis=0, keepdims=True) for scores in found]
        )
        if not causal:
            peak, total, summed = (ref[g, :, columns] for ref in refs)
            new_peak = jnp.maximum(peak, new_peak)
            rescale = jnp.exp2((peak - new_peak) * exp2_scale)
            new_total, new_summed = total * rescale, summed * rescale
        else:
            new_total, new_summed = 0.0, 0.0
        for scores, (_, v) in zip(found, tiles):
            expo = jnp.exp2((scores - new_peak) * exp2_scale)
            v = v[: (n + 1) * width] if causal else v[...]
            new_total += jnp.sum(expo, axis=0, keepdims=True)
            new_summed += lax.dot_general(
                v, expo.astype(BF), (((0,), (0,)), ((), ())), preferred_element_type=F32
            )
        for ref, part in zip(refs, (new_peak, new_total, new_summed)):
            ref[g, :, columns] = part


def own_kernel(where_ref, q_ref, ok, ov, *outs):
    refs, where_out = outs[:3], outs[3]
    for n in range(3):
        where_out[n] = where_ref[n]
    absorb(refs, q_ref, [(ok, ov)], causal=True)


def middle_kernel(where_ref, q_ref, p_ref, t_ref, s_ref, ak, av, bk, bv, nk, nv, mk, mv, *refs):
    zh, blk = where_ref[1], where_ref[2]
    for ref, before in zip(refs, (p_ref, t_ref, s_ref)):
        ref[...] = before[...]

    @pl.when(blk > 0)
    def _():
        tile = 512

        def step(t, _):
            at = pl.ds(pl.multiple_of(t * tile, tile), tile)
            absorb(refs, q_ref, [(nk[at, :], nv[at, :]), (mk[at, :], mv[at, :])])
            return 0

        lax.fori_loop(0, nk.shape[0] // tile, step, 0)

    @pl.when(jnp.logical_and(zh > 0, zh < 3))
    def _():
        absorb(refs, q_ref, [(ak, av)])

    @pl.when(zh == 3)
    def _():
        absorb(refs, q_ref, [(ak, av), (bk, bv)])


def last_kernel(where_ref, q_ref, peak_ref, total_ref, summed_ref, ak, av, bk, bv, out_ref, *own):
    for mine, ref in zip(own, (peak_ref, total_ref, summed_ref)):
        mine[...] = ref[...]

    @pl.when(where_ref[1] > 1)
    def _():
        absorb(own, q_ref, [(ak, av), (bk, bv)])

    for g in range(2):
        out_ref[:, g * HD : (g + 1) * HD] = (own[2][g] / own[1][g]).T.astype(BF)


def head_specs(rows):
    return [
        pl.BlockSpec((rows, HD), lambda h, w: (0, h)),
        pl.BlockSpec((rows, HD), lambda h, w: (0, 2 + h)),
    ]


def state_shapes(heads, rows):
    return [(heads, 1, rows), (heads, 1, rows), (heads, HD, rows)]


def state_specs(rows):
    return [pl.BlockSpec(shape, lambda h, w: (h, 0, 0)) for shape in state_shapes(2, rows)]


def attention_call(body, name, where, q, state, parts, out_specs, out_shape, scratch, share=1):
    rows = q.shape[0]
    keys = sum(part.shape[0] for part in parts)
    in_specs = [pl.BlockSpec((rows, 2 * HD), lambda h, w: (0, h))]
    if state:
        in_specs += state_specs(rows)
    operands = [q, *state]
    for part in parts:
        in_specs += head_specs(part.shape[0])
        operands += [part, part]
    return pl.pallas_call(
        body,
        grid_spec=pltpu.PrefetchScalarGridSpec(
            num_scalar_prefetch=1,
            grid=(2,),
            in_specs=in_specs,
            out_specs=out_specs,
            scratch_shapes=scratch,
        ),
        out_shape=out_shape,
        compiler_params=pltpu.CompilerParams(vmem_limit_bytes=40 * 1024 * 1024),
        cost_estimate=pl.CostEstimate(
            flops=4 * 4 * rows * keys * HD // share, bytes_accessed=(8 << 20) // share, transcendentals=4 * rows * keys // share
        ),
        name=name,
    )(where, *operands)


def own_part(where, q, own):
    rows = q.shape[0]
    return attention_call(
        own_kernel,
        "own_attention",
        where,
        q,
        (),
        (own,),
        state_specs(rows) + [pl.BlockSpec(memory_space=pltpu.SMEM)],
        [jax.ShapeDtypeStruct(shape, F32) for shape in state_shapes(4, rows)]
        + [jax.ShapeDtypeStruct((3,), jnp.int32)],
        [],
        64,
    )


def middle(where, q, state, parts):
    rows = q.shape[0]
    return attention_call(
        middle_kernel,
        "middle_attention",
        where,
        q,
        state,
        parts,
        state_specs(rows),
        [jax.ShapeDtypeStruct(shape, F32) for shape in state_shapes(4, rows)],
        [],
    )


def last(where, q, state, parts):
    rows = q.shape[0]
    return attention_call(
        last_kernel,
        "last_attention",
        where,
        q,
        state,
        parts,
        pl.BlockSpec((rows, 2 * HD), lambda h, w: (0, h)),
        jax.ShapeDtypeStruct((rows, 4 * HD), BF),
        [pltpu.VMEM(shape, F32) for shape in state_shapes(2, rows)],
    )


def device_index(zl, y, c, zh, x):
    return (((zl * 4 + y) * 2 + c) * 4 + zh) * 4 + x


def send(block, move):
    places = itertools.product(*(range(size) for size in SIZES))
    moves = [(place, move(*place)) for place in places]
    return lax.ppermute(
        block, AXES, [(device_index(*place), device_index(*to)) for place, to in moves if to is not None]
    )


def of_heads(block):
    width = block.shape[1] // 2
    return jnp.concatenate(
        [
            jnp.concatenate(
                [block[:, n * 256 : (n + 1) * 256], block[:, width + n * 256 : width + (n + 1) * 256]], 1
            )
            for n in range(HEADS_X)
        ],
        0,
    )


def local(queries, keys, values):
    zl, y, c, zh, x = (lax.axis_index(name) for name in AXES)
    blk = (zl * SIZES[1] + y) * SIZES[2] + c
    where = jnp.stack([x, zh, blk]).astype(jnp.int32)
    always = blk < 32
    raw = jnp.concatenate([keys, values], 1)

    own = exchange(of_heads(raw), "x")
    rows = own.shape[0]
    def step(body, *operands):
        shapes = jax.eval_shape(body, *operands)
        return lax.cond(
            always,
            body,
            lambda *_: jax.tree.map(lambda one: jnp.zeros(one.shape, one.dtype), shapes),
            *operands,
        )

    part = raw.shape[0] // 4
    held = raw[:part]
    for to in range(1, 4):
        got = send(
            raw[to * part : (to + 1) * part],
            lambda zl, y, c, zh, x: (0, to, 0, zh, x) if (zl, y, c) == (0, 0, 0) else None,
        )
        held = jnp.where(y == to, got, held)

    def doubled(held, swap):
        got = send(held, lambda zl, y, c, zh, x: (0, y, 0, swap[zh], x) if (zl, c) == (0, 0) else None)
        return jnp.concatenate([held, got], 0)

    def over_z(held, own):
        held = doubled(doubled(held, (1, 0, 3, 2)), (3, 2, 1, 0))
        first = lambda zl, c: (zl, c) == (0, 0)
        two = send(held, lambda zl, y, c, zh, x: (2, y, 0, zh, x) if first(zl, c) else None)
        one = send(held, lambda zl, y, c, zh, x: (1, y, 0, zh, x) if first(zl, c) else None)
        three = send(held, lambda zl, y, c, zh, x: (3, y, 0, (zh + 3) % 4, x) if first(zl, c) else None)
        strip = jnp.where(zl == 0, held, jnp.where(zl == 1, one, jnp.where(zl == 2, two, three)))
        half = strip.shape[0] // 2
        moved = lax.ppermute(strip[half:], "c", [(0, 1)])
        return jnp.where(c == 0, strip[:half], moved), own

    strip, own = step(over_z, held, own)

    half = rows // 2
    got_b = lax.ppermute(own, "zh", [(0, 3), (1, 0)])
    got_a = lax.ppermute(own, "zh", [(0, 1), (1, 2), (2, 3)])

    def whole_anchor(strip, where):
        here = gathered(of_heads(strip), ("y", "x"), 4)
        return here, lax.ppermute(here, "c", [(0, 1), (1, 0)]), where

    here, there, where = step(whole_anchor, strip, where)
    q = exchange(
        jnp.concatenate([queries[:, n * 512 : (n + 1) * 512] for n in range(HEADS_X)], 0), "x"
    )
    *state, where = own_part(where, q, own)
    arrived = where[2] >= 0
    got_a2 = lax.ppermute(jnp.where(arrived, got_a[:half], own[:half]), "zh", [(1, 2), (2, 3)])
    got_b2 = lax.ppermute(jnp.where(arrived, got_b[half:], own[half:]), "zh", [(3, 2), (0, 3)])
    state = middle(where, q, state, (got_a, got_b, here, there))
    out = exchange(last(where, q, state, (got_a2, got_b2)), "x")
    width = rows // HEADS_X
    return jnp.concatenate([out[n * width : (n + 1) * width] for n in range(HEADS_X)], 1)


def solution(mesh):
    spec = P(AXES, None)
    split = jax.sharding.Mesh(mesh.devices.reshape(SIZES), AXES)
    return jax.shard_map(local, mesh=split, in_specs=(spec,) * 3, out_specs=spec, check_vma=False)
```

```python
import functools
import itertools

import jax
import jax.numpy as jnp
from jax import lax
from jax.experimental import pallas as pl
from jax.experimental.pallas import tpu as pltpu
from jax.sharding import PartitionSpec as P

HD = 128
BF = jnp.bfloat16
F32 = jnp.float32
masked_value = -1e30
exp2_scale = 0.08838834764831845 * 1.4426950408889634

AXES = ("zl", "y", "c", "zh", "x")
SIZES = (4, 4, 2, 4, 4)
HEADS_X = 4


def exchange(block, axes):
    return lax.all_to_all(block, axes, split_axis=0, concat_axis=0, tiled=True)


def gathered(block, axis, size):
    return exchange(jnp.concatenate([block] * size, 0), axis)


def absorb(refs, q_ref, tiles, causal=False):
    rows = q_ref.shape[0]
    width = rows // 2
    chains = [(g, n) for g in range(2) for n in range(2)]

    def scores_of(chain):
        g, n = chain
        q = q_ref[n * width : (n + 1) * width, g * HD : (g + 1) * HD]
        found = []
        for k, _ in tiles:
            k = k[: (n + 1) * width] if causal else k[...]
            found.append(lax.dot_general(k, q, (((1,), (1,)), ((), ())), preferred_element_type=F32))
        if causal:
            key_at = lax.broadcasted_iota(jnp.int32, found[0].shape, 0)
            query_at = lax.broadcasted_iota(jnp.int32, found[0].shape, 1) + n * width
            found = [jnp.where(key_at <= query_at, found[0], masked_value)]
        return found

    following = scores_of(chains[0])
    for at, (g, n) in enumerate(chains):
        found = following
        if at + 1 < len(chains):
            following = scores_of(chains[at + 1])
        columns = slice(n * width, (n + 1) * width)
        new_peak = functools.reduce(
            jnp.maximum, [jnp.max(scores, axis=0, keepdims=True) for scores in found]
        )
        if not causal:
            peak, total, summed = (ref[g, :, columns] for ref in refs)
            new_peak = jnp.maximum(peak, new_peak)
            rescale = jnp.exp2((peak - new_peak) * exp2_scale)
            new_total, new_summed = total * rescale, summed * rescale
        else:
            new_total, new_summed = 0.0, 0.0
        for scores, (_, v) in zip(found, tiles):
            expo = jnp.exp2((scores - new_peak) * exp2_scale)
            v = v[: (n + 1) * width] if causal else v[...]
            new_total += jnp.sum(expo, axis=0, keepdims=True)
            new_summed += lax.dot_general(
                v, expo.astype(BF), (((0,), (0,)), ((), ())), preferred_element_type=F32
            )
        for ref, part in zip(refs, (new_peak, new_total, new_summed)):
            ref[g, :, columns] = part


def own_kernel(where_ref, q_ref, ok, ov, *outs):
    refs, where_out = outs[:3], outs[3]
    for n in range(3):
        where_out[n] = where_ref[n]
    absorb(refs, q_ref, [(ok, ov)], causal=True)


def middle_kernel(where_ref, q_ref, p_ref, t_ref, s_ref, ak, av, bk, bv, nk, nv, mk, mv, *refs):
    zh, blk = where_ref[1], where_ref[2]
    for ref, before in zip(refs, (p_ref, t_ref, s_ref)):
        ref[...] = before[...]

    @pl.when(blk > 0)
    def _():
        tile = 512

        def step(t, _):
            at = pl.ds(pl.multiple_of(t * tile, tile), tile)
            absorb(refs, q_ref, [(nk[at, :], nv[at, :]), (mk[at, :], mv[at, :])])
            return 0

        lax.fori_loop(0, nk.shape[0] // tile, step, 0)

    @pl.when(jnp.logical_and(zh > 0, zh < 3))
    def _():
        absorb(refs, q_ref, [(ak, av)])

    @pl.when(zh == 3)
    def _():
        absorb(refs, q_ref, [(ak, av), (bk, bv)])


def last_kernel(where_ref, q_ref, peak_ref, total_ref, summed_ref, ak, av, bk, bv, out_ref, *own):
    for mine, ref in zip(own, (peak_ref, total_ref, summed_ref)):
        mine[...] = ref[...]

    @pl.when(where_ref[1] > 1)
    def _():
        absorb(own, q_ref, [(ak, av), (bk, bv)])

    for g in range(2):
        out_ref[:, g * HD : (g + 1) * HD] = (own[2][g] / own[1][g]).T.astype(BF)


def head_specs(rows):
    return [
        pl.BlockSpec((rows, HD), lambda h, w: (0, h)),
        pl.BlockSpec((rows, HD), lambda h, w: (0, 2 + h)),
    ]


def state_shapes(heads, rows):
    return [(heads, 1, rows), (heads, 1, rows), (heads, HD, rows)]


def state_specs(rows):
    return [pl.BlockSpec(shape, lambda h, w: (h, 0, 0)) for shape in state_shapes(2, rows)]


def attention_call(body, name, where, q, state, parts, out_specs, out_shape, scratch, share=1):
    rows = q.shape[0]
    keys = sum(part.shape[0] for part in parts)
    in_specs = [pl.BlockSpec((rows, 2 * HD), lambda h, w: (0, h))]
    if state:
        in_specs += state_specs(rows)
    operands = [q, *state]
    for part in parts:
        in_specs += head_specs(part.shape[0])
        operands += [part, part]
    return pl.pallas_call(
        body,
        grid_spec=pltpu.PrefetchScalarGridSpec(
            num_scalar_prefetch=1,
            grid=(2,),
            in_specs=in_specs,
            out_specs=out_specs,
            scratch_shapes=scratch,
        ),
        out_shape=out_shape,
        compiler_params=pltpu.CompilerParams(vmem_limit_bytes=40 * 1024 * 1024),
        cost_estimate=pl.CostEstimate(
            flops=4 * 4 * rows * keys * HD // share, bytes_accessed=(8 << 20) // share, transcendentals=4 * rows * keys // share
        ),
        name=name,
    )(where, *operands)


def own_part(where, q, own):
    rows = q.shape[0]
    return attention_call(
        own_kernel,
        "own_attention",
        where,
        q,
        (),
        (own,),
        state_specs(rows) + [pl.BlockSpec(memory_space=pltpu.SMEM)],
        [jax.ShapeDtypeStruct(shape, F32) for shape in state_shapes(4, rows)]
        + [jax.ShapeDtypeStruct((3,), jnp.int32)],
        [],
        64,
    )


def middle(where, q, state, parts):
    rows = q.shape[0]
    return attention_call(
        middle_kernel,
        "middle_attention",
        where,
        q,
        state,
        parts,
        state_specs(rows),
        [jax.ShapeDtypeStruct(shape, F32) for shape in state_shapes(4, rows)],
        [],
        10**6,
    )


def last(where, q, state, parts):
    rows = q.shape[0]
    return attention_call(
        last_kernel,
        "last_attention",
        where,
        q,
        state,
        parts,
        pl.BlockSpec((rows, 2 * HD), lambda h, w: (0, h)),
        jax.ShapeDtypeStruct((rows, 4 * HD), BF),
        [pltpu.VMEM(shape, F32) for shape in state_shapes(2, rows)],
    )


def device_index(zl, y, c, zh, x):
    return (((zl * 4 + y) * 2 + c) * 4 + zh) * 4 + x


def send(block, move):
    places = itertools.product(*(range(size) for size in SIZES))
    moves = [(place, move(*place)) for place in places]
    return lax.ppermute(
        block, AXES, [(device_index(*place), device_index(*to)) for place, to in moves if to is not None]
    )


def of_heads(block):
    width = block.shape[1] // 2
    return jnp.concatenate(
        [
            jnp.concatenate(
                [block[:, n * 256 : (n + 1) * 256], block[:, width + n * 256 : width + (n + 1) * 256]], 1
            )
            for n in range(HEADS_X)
        ],
        0,
    )


def local(queries, keys, values):
    zl, y, c, zh, x = (lax.axis_index(name) for name in AXES)
    blk = (zl * SIZES[1] + y) * SIZES[2] + c
    where = jnp.stack([x, zh, blk]).astype(jnp.int32)
    always = blk < 32
    raw = jnp.concatenate([keys, values], 1)

    own = exchange(of_heads(raw), "x")
    rows = own.shape[0]
    def step(body, *operands):
        shapes = jax.eval_shape(body, *operands)
        return lax.cond(
            always,
            body,
            lambda *_: jax.tree.map(lambda one: jnp.zeros(one.shape, one.dtype), shapes),
            *operands,
        )

    part = raw.shape[0] // 4
    held = raw[:part]
    for to in range(1, 4):
        got = send(
            raw[to * part : (to + 1) * part],
            lambda zl, y, c, zh, x: (0, to, 0, zh, x) if (zl, y, c) == (0, 0, 0) else None,
        )
        held = jnp.where(y == to, got, held)

    def doubled(held, swap):
        got = send(held, lambda zl, y, c, zh, x: (0, y, 0, swap[zh], x) if (zl, c) == (0, 0) else None)
        return jnp.concatenate([held, got], 0)

    def over_z(held, own):
        held = doubled(doubled(held, (1, 0, 3, 2)), (3, 2, 1, 0))
        first = lambda zl, c: (zl, c) == (0, 0)
        two = send(held, lambda zl, y, c, zh, x: (2, y, 0, zh, x) if first(zl, c) else None)
        one = send(held, lambda zl, y, c, zh, x: (1, y, 0, zh, x) if first(zl, c) else None)
        three = send(held, lambda zl, y, c, zh, x: (3, y, 0, (zh + 3) % 4, x) if first(zl, c) else None)
        strip = jnp.where(zl == 0, held, jnp.where(zl == 1, one, jnp.where(zl == 2, two, three)))
        half = strip.shape[0] // 2
        moved = lax.ppermute(strip[half:], "c", [(0, 1)])
        return jnp.where(c == 0, strip[:half], moved), own

    strip, own = step(over_z, held, own)

    half = rows // 2
    got_b = lax.ppermute(own, "zh", [(0, 3), (1, 0)])
    got_a = lax.ppermute(own, "zh", [(0, 1), (1, 2), (2, 3)])

    def whole_anchor(strip, where):
        here = gathered(of_heads(strip), ("y", "x"), 4)
        return here, lax.ppermute(here, "c", [(0, 1), (1, 0)]), where

    here, there, where = step(whole_anchor, strip, where)
    arrived = where[2] >= 0
    got_a2 = lax.ppermute(jnp.where(arrived, got_a[:half], own[:half]), "zh", [(1, 2), (2, 3)])
    got_b2 = lax.ppermute(jnp.where(arrived, got_b[half:], own[half:]), "zh", [(3, 2), (0, 3)])
    def queries_and_own(where):
        q = exchange(
            jnp.concatenate([queries[:, n * 512 : (n + 1) * 512] for n in range(HEADS_X)], 0), "x"
        )
        return q, *own_part(where, q, own)

    q, *state, where = step(queries_and_own, where)
    state = middle(where, q, state, (got_a, got_b, here, there))
    out = exchange(last(where, q, state, (got_a2, got_b2)), "x")
    width = rows // HEADS_X
    return jnp.concatenate([out[n * width : (n + 1) * width] for n in range(HEADS_X)], 1)


def solution(mesh):
    spec = P(AXES, None)
    split = jax.sharding.Mesh(mesh.devices.reshape(SIZES), AXES)
    return jax.shard_map(local, mesh=split, in_specs=(spec,) * 3, out_specs=spec, check_vma=False)
```
